32 devices in a mesh: depth: 4 (over x, core), row: 4 (over z), col: 2 (over y).
Axes of the slice: x: 2, y: 2, z: 4, core: 2. Of those that a mesh axis runs over, the one named last changes fastest.
Arguments:
- density: float32 [4096, 4096], P('row', ('depth', 'col')), as said below
- pattern: int32 [64, 64], replicated, may hold values from 0 to 1, as said below
- filters: int32 [4, 64, 64], replicated, may hold values from 0 to 1, as said below
Outputs:
- purified: float32 [4096, 4096], P('row', ('depth', 'col'))
The draws below stay inside these ranges and needn't reach their ends.
Inputs may be any that keep to these rules, and one draw needn't show every extreme that they name: density is symmetric. `pattern`: symmetric 0/1 block table with every diagonal block set. `filters`: each table is a symmetric 0/1 block table with every diagonal block set.
All inputs are finite; a program needn't handle non-finite values.
Results may differ from the reference program's by a relative error of at most 0.007.
Values may be sent and summed in bfloat16 or wider, within the bound.
A program may use at most 64 MiB of HBM per device.

```python
import math
import jax
import jax.numpy as jnp

BLK = 64
NB = 64
PURIFY = 2
ORDER = 4096


def block_keep(key, near_pct, far_pct):
    tip_key, fill_key = jax.random.split(key)
    tip_block = jax.random.randint(tip_key, (), 0, NB)
    indices = jnp.arange(NB)
    closeby = jnp.abs(indices - tip_block) < max(NB // 4, 1)
    nearby = closeby[:, None] & closeby[None, :] | (jnp.abs(indices[:, None] - indices[None, :]) <= 2)
    rolled = jax.random.randint(fill_key, (NB, NB), 0, 100)
    kept_blocks = rolled < jnp.where(nearby, near_pct, far_pct)
    kept_blocks = kept_blocks | kept_blocks.T | (indices[:, None] == indices[None, :])
    return kept_blocks.astype(jnp.int32)


def draw_pattern(key, part):
    return block_keep(jax.random.fold_in(key, 11), 90, 45)


def draw_filters(key, part):
    tables = [block_keep(jax.random.fold_in(key, 100 + number), 97, 70) for number in range(2 * PURIFY)]
    return jnp.stack(tables)


def draw_density(key, part):
    noise_key, diag_key = jax.random.split(jax.random.fold_in(key, 7), 2)
    indices = jnp.arange(ORDER)
    random_part = jax.random.normal(noise_key, (ORDER, ORDER), jnp.float32)
    diagonal = jax.random.uniform(diag_key, (ORDER,), jnp.float32, 0.25, 0.75)
    symmetric = (random_part + random_part.T) * (0.25 / math.sqrt(2.0 * ORDER))
    return jnp.where(indices[:, None] == indices[None, :], diagonal[:, None], symmetric)


def setup_inputs(seed: int = 0) -> dict:
    seeds = jax.random.split(jax.random.key(seed), 4)
    return {
        "density": draw_density(jax.random.fold_in(seeds[3], 71), 0),
        "pattern": draw_pattern(jax.random.fold_in(seeds[3], 71), 0),
        "filters": draw_filters(jax.random.fold_in(seeds[3], 71), 0),
    }


def expand(keep_table):
    shaped = jnp.broadcast_to(keep_table.astype(jnp.float32)[:, None, :, None], (NB, BLK, NB, BLK))
    return shaped.reshape(ORDER, ORDER)


def reference(density, pattern, filters):
    current = density * expand(pattern)
    for round_index in range(PURIFY):
        operand = current.astype(jnp.bfloat16)
        square = jnp.dot(operand, operand, preferred_element_type=jnp.float32) * expand(filters[2 * round_index])
        cubic = jnp.dot(square.astype(jnp.bfloat16), operand, preferred_element_type=jnp.float32) * expand(filters[2 * round_index + 1])
        current = 3.0 * square - 2.0 * cubic
    return current
```

```python
import functools

import jax
import jax.numpy as jnp
from jax import lax
from jax.experimental import pallas as pl
from jax.experimental.pallas import tpu as pltpu
from jax.sharding import PartitionSpec as P

BLK = 64
PURIFY = 2
CORES = 2
LANES = 128
MESH = pl.DeviceIdType.MESH


def kernel(dims, dens, pat_in, filt_in, out, a_row, a_col, s_row, sq, acc, mask, pat, filt,
           z_send, z_recv, a_send, a_recv, af_send, af_recv,
           s_send, s_recv, sf_send, sf_recv, o_sem, t_sem):
    nd, nr, nc, h, w, tm, cuts = dims
    Q = len(cuts)
    G = w // LANES
    T = h // tm
    nx = nd // CORES
    m = h // w
    rb, sb = h // BLK, w // BLK
    d, r, c = lax.axis_index("depth"), lax.axis_index("row"), lax.axis_index("col")
    x, core = d // CORES, d % CORES
    sib = x * CORES + (1 - core)
    me = d * nc + c
    peers = [(px, pc) for px in range(nx) for pc in range(nc) if px or pc]
    direct = [p for p, (px, pc) in enumerate(peers) if not (px and pc)]
    bent = [p for p, (px, pc) in enumerate(peers) if px and pc]

    def dev(dd, rr, cc):
        return (dd, rr, cc)

    def peer_to(p):
        px, pc = peers[p]
        return ((x + px) % nx) * CORES + core, (c + pc) % nc

    def peer_from(p, k):
        px, pc = peers[p]
        return ((x + nx - px) % nx) * CORES + k, (c + nc - pc) % nc

    def load(t):
        rows = pl.ds(pl.multiple_of(t * tm, tm), tm)
        return pltpu.make_async_copy(dens.at[rows, :], acc.at[rows, :], o_sem.at[t])

    tables = [pltpu.make_async_copy(pat_in, pat, t_sem.at[0]), pltpu.make_async_copy(filt_in, filt, t_sem.at[1])]
    tables[0].start()
    for t in range(T):
        load(t).start()
    tables[1].start()
    bar = pltpu.get_barrier_semaphore()
    for p in direct:
        dd, cc = peer_to(p)
        pl.semaphore_signal(bar, inc=1, device_id=dev(dd, r, cc), device_id_type=MESH)
    pl.semaphore_signal(bar, inc=1, device_id=dev(sib, r, c), device_id_type=MESH)

    @pl.when(r > 0)
    def _():
        pl.semaphore_signal(bar, inc=1, device_id=dev(d, r - 1, c), device_id_type=MESH)

    @pl.when(r < nr - 1)
    def _():
        pl.semaphore_signal(bar, inc=1, device_id=dev(d, r + 1, c), device_id_type=MESH)

    tb = tm // BLK
    slot = lax.broadcasted_iota(jnp.int32, (T * 8, pat.shape[0]), 0)
    r_pick = (slot // 8 * tb + slot % 8 + r * rb
              == lax.broadcasted_iota(jnp.int32, (T * 8, pat.shape[0]), 1)).astype(jnp.float32)
    c_pick = ((lax.broadcasted_iota(jnp.int32, (pat.shape[1], w), 1) // BLK + me * sb)
              == lax.broadcasted_iota(jnp.int32, (pat.shape[1], w), 0)).astype(jnp.float32)

    def expand(k, table):
        rows = jnp.dot(r_pick, table.astype(jnp.float32), preferred_element_type=jnp.float32)
        mask[k] = jnp.dot(rows, c_pick, preferred_element_type=jnp.float32)

    tables[0].wait()
    expand(0, pat[...])

    def tile_mask(k, t, g0, g1):
        n = (g1 - g0) * LANES
        mk = mask[k, pl.ds(pl.multiple_of(t * 8, 8), 8), g0 * LANES:g1 * LANES][:tb]
        return jnp.broadcast_to(mk[:, None, :], (tb, BLK, n)).reshape(tm, n)

    def rows_of(t):
        return pl.ds(pl.multiple_of(t * tm, tm), tm)

    def operand(t, groups):
        for g in groups:
            v = (acc[rows_of(t), g * LANES:(g + 1) * LANES] * tile_mask(0, t, g, g + 1)).astype(jnp.bfloat16)
            a_col[0, r, g, rows_of(t), :] = v
            a_row[0, me, g, rows_of(t), :] = v

    @pl.loop(0, T)
    def _(t):
        load(t).wait()
        operand(t, range(*cuts[0]))

    near = jnp.minimum(r, 1) + jnp.minimum(nr - 1 - r, 1)
    for n in range(3):
        @pl.when(near == n)
        def _():
            pl.semaphore_wait(bar, len(direct) + 1 + n)

    def z_copy(s, q, src, up):
        ref = a_col.at[s, src, cuts[q][0]:cuts[q][1]]
        return pltpu.make_async_remote_copy(
            src_ref=ref, dst_ref=ref, send_sem=z_send.at[s, q, src, up],
            recv_sem=z_recv.at[s, q, src],
            device_id=dev(d, r + 1 if up else r - 1, c), device_id_type=MESH)

    def z_own(s, q, op):
        @pl.when(r < nr - 1)
        def _():
            getattr(z_copy(s, q, r, 1), op)()

        @pl.when(r > 0)
        def _():
            getattr(z_copy(s, q, r, 0), op)()

    def pass_down(s, q, dist):
        z_copy(s, q, r + dist, 1).wait_recv()
        z_copy(s, q, r + dist, 0).start()

    def pass_up(s, q, dist):
        z_copy(s, q, r - dist, 0).wait_recv()
        z_copy(s, q, r - dist, 1).start()

    def z_fwd(s, q, dist, outer):
        for edge in (0, 1):
            if edge == outer:
                @pl.when((r + dist < nr) & (r > 0) & ((r + dist == nr - 1) == bool(edge)))
                def _():
                    pass_down(s, q, dist)

                @pl.when((r - dist >= 0) & (r < nr - 1) & ((r - dist == 0) == bool(edge)))
                def _():
                    pass_up(s, q, dist)

    def z_inner(s, q):
        for dist in range(1, nr - 1):
            z_fwd(s, q, dist, 0)

    def z_outer(s, q):
        for dist in range(1, nr - 1):
            z_fwd(s, q, dist, 1)

    def z_wait(s, q):
        for dist in range(1, nr):
            @pl.when((r + dist < nr) & (r == 0))
            def _():
                z_copy(s, q, r + dist, 1).wait_recv()

            @pl.when((r - dist >= 0) & (r == nr - 1))
            def _():
                z_copy(s, q, r - dist, 0).wait_recv()

    def z_drain(s, q):
        z_own(s, q, "wait_send")
        for dist in range(1, nr - 1):
            @pl.when((r + dist < nr) & (r > 0))
            def _():
                z_copy(s, q, r + dist, 0).wait_send()

            @pl.when((r - dist >= 0) & (r < nr - 1))
            def _():
                z_copy(s, q, r - dist, 1).wait_send()

    def ac(ref, ss, rs, to):
        return pltpu.make_async_remote_copy(
            src_ref=ref, dst_ref=ref, send_sem=ss, recv_sem=rs,
            device_id=dev(to[0], r, to[1]), device_id_type=MESH)

    class Gather:
        def __init__(self, view, sems, tag):
            self.view, self.sems, self.tag = view, sems, tag

        def sem(self, n, t, *at):
            return self.sems[n].at[(*self.tag, t, *at)]

        def block(self, p, k, t):
            dd, cc = peer_from(p, k)
            return self.view(dd * nc + cc, t * tm, tm)

        def half(self, dd, cc, t, i):
            return self.view(dd * nc + cc, t * tm + i * (tm // 2), tm // 2)

        def path(self, ref, p, t, i, to):
            return ac(ref, self.sem(0, t, p, i), self.sem(1, t, p, i), to)

        def own(self, p, t):
            return self.path(self.view(me, t * tm, tm), p, t, 0, peer_to(p))

        def got(self, p, t, i=None):
            if i is None:
                return self.path(self.block(p, core, t), p, t, 0, peer_to(p))
            dd, cc = peer_from(p, core)
            return self.path(self.half(dd, cc, t, i), p, t, i, peer_to(p))

        def turn(self, p, t, i):
            px, pc = peers[p]
            if i == 0:
                ref = self.half(((x + nx - px) % nx) * CORES + core, c, t, 0)
                to = (d, (c + pc) % nc)
            else:
                ref = self.half(d, (c + nc - pc) % nc, t, 1)
                to = (((x + px) % nx) * CORES + core, c)
            return self.path(ref, p, t, i, to)

        def fwd(self, p, t):
            ref = self.view(me, t * tm, tm) if p == len(peers) else self.block(p, core, t)
            return ac(ref, self.sem(2, t, p), self.sem(3, t, p), (sib, c))

        def fgot(self, p, t):
            ref = self.view(sib * nc + c, t * tm, tm) if p == len(peers) else self.block(p, 1 - core, t)
            return ac(ref, self.sem(2, t, p), self.sem(3, t, p), (sib, c))

        def begin(self, t):
            for p in direct:
                self.own(p, t).start()
            self.fwd(len(peers), t).start()

        def hop(self, t):
            for q in direct:
                self.got(q, t).wait_recv()
                for p in bent:
                    if peers[q] == (peers[p][0], 0):
                        self.turn(p, t, 0).start()
                    if peers[q] == (0, peers[p][1]):
                        self.turn(p, t, 1).start()
            for q in direct:
                self.fwd(q, t).start()

        def relay(self, t):
            for p in bent:
                self.got(p, t, 0).wait_recv()
                self.got(p, t, 1).wait_recv()
                self.fwd(p, t).start()

        def finish(self, t):
            for p in range(len(peers) + 1):
                self.fgot(p, t).wait_recv()

        def drain(self, t):
            for p in direct:
                self.own(p, t).wait_send()
            for p in bent:
                self.turn(p, t, 0).wait_send()
                self.turn(p, t, 1).wait_send()
            for p in range(len(peers) + 1):
                self.fwd(p, t).wait_send()

    def span(lo, n):
        return pl.ds(lo if isinstance(lo, int) else pl.multiple_of(lo, tm // 2), n)

    ga = [Gather(lambda j, lo, n, s=s: a_row.at[s, j, :, span(lo, n)],
                 (a_send, a_recv, af_send, af_recv), (s,)) for s in range(PURIFY)]
    gs = [[Gather(lambda j, lo, n, s=s, q=q: s_row.at[s, j, cuts[q][0]:cuts[q][1], span(lo, n)],
                  (s_send, s_recv, sf_send, sf_recv), (s, q)) for q in range(Q)] for s in range(PURIFY)]

    def product(left, s, t, groups, g0, g1):
        cells = [(j, g) for j in range(nd * nc) for g in groups]
        tot = None
        for i in range(0, len(cells), 2):
            pair = cells[i:i + 2]
            lhs = jnp.concatenate([left[s, j, g, rows_of(t), :] for j, g in pair], axis=1)
            cols = []
            for n in range(g0, g1):
                los = [(j // m, (j % m) * w + g * LANES) for j, g in pair]
                if len(los) == 2 and los[1] == (los[0][0], los[0][1] + LANES):
                    cols.append(a_col[s, los[0][0], n, los[0][1]:los[0][1] + 2 * LANES, :])
                else:
                    cols.append(jnp.concatenate([a_col[s, b, n, lo:lo + LANES, :] for b, lo in los], axis=0))
            part = jnp.dot(lhs, jnp.concatenate(cols, axis=1), preferred_element_type=jnp.float32)
            tot = part if tot is None else tot + part
        return tot

    def square(s, q, t):
        g0, g1 = cuts[q]
        tot = product(a_row, s, t, range(G), g0, g1) * tile_mask(2 * s + 1, t, g0, g1)
        sq[rows_of(t), g0 * LANES:g1 * LANES] = tot
        v = tot.astype(jnp.bfloat16)
        for g in range(g0, g1):
            s_row[s, me, g, rows_of(t), :] = v[:, (g - g0) * LANES:(g - g0 + 1) * LANES]

    def put(t):
        return pltpu.make_async_copy(acc.at[rows_of(t), :], out.at[rows_of(t), :], o_sem.at[t])

    def cubic(s, k, t, g0, g1):
        cols = slice(g0 * LANES, g1 * LANES)
        tot = product(s_row, s, t, range(*cuts[k]), g0, g1)
        if k > 0:
            tot = tot + acc[rows_of(t), cols]
        if k < Q - 1:
            acc[rows_of(t), cols] = tot
            return
        cur = 3.0 * sq[rows_of(t), cols] - 2.0 * (tot * tile_mask(2 * s + 2, t, g0, g1))
        if s < PURIFY - 1:
            v = cur.astype(jnp.bfloat16)
            for g in range(g0, g1):
                part = v[:, (g - g0) * LANES:(g - g0 + 1) * LANES]
                a_col[s + 1, r, g, rows_of(t), :] = part
                a_row[s + 1, me, g, rows_of(t), :] = part
        else:
            acc[rows_of(t), cols] = cur

    wide = [(g, min(g + 2, G)) for g in range(0, G, 2)]
    ready = [[] for _ in range(Q)]
    for k in range(Q - 1):
        for g0, g1 in wide:
            ready[next(q for q in range(k + 1, Q) if q == Q - 1 or cuts[q][1] >= g1)].append((k, (g0, g1)))
    z_own(0, 0, "start")

    @pl.loop(0, T)
    def _(t):
        operand(t, range(cuts[0][1], G))
        ga[0].begin(t)

    tables[1].wait()
    for k in range(filt.shape[0]):
        expand(k + 1, filt[k])
    for s in range(PURIFY):
        ga[s].hop(0)
        z_inner(s, 0)
        if Q > 1:
            z_own(s, 1, "start")
        for t in range(1, T):
            ga[s].hop(t)
        if Q > 1:
            z_inner(s, 1)
        z_outer(s, 0)
        for t in range(T):
            ga[s].relay(t)
        if Q > 1:
            z_outer(s, 1)
        if Q > 2:
            z_own(s, 2, "start")
        z_wait(s, 0)

        @pl.loop(0, T)
        def _(t):
            ga[s].finish(t)
            square(s, 0, t)
            gs[s][0].begin(t)

        for q in range(1, Q):
            if q + 1 < Q:
                z_inner(s, q + 1)
                z_outer(s, q + 1)
                if q + 2 < Q:
                    z_own(s, q + 2, "start")

            @pl.loop(0, T)
            def _(t):
                gs[s][q - 1].hop(t)

            z_wait(s, q)

            @pl.loop(0, T)
            def _(t):
                square(s, q, t)
                gs[s][q].begin(t)

            @pl.loop(0, T)
            def _(t):
                gs[s][q - 1].relay(t)

            @pl.loop(0, T)
            def _(t):
                gs[s][q - 1].finish(t)
                for k, (g0, g1) in ready[q]:
                    cubic(s, k, t, g0, g1)

        @pl.loop(0, T)
        def _(t):
            gs[s][Q - 1].hop(t)

        @pl.loop(0, T)
        def _(t):
            gs[s][Q - 1].relay(t)
            gs[s][Q - 1].finish(t)
            for g0, g1 in wide:
                cubic(s, Q - 1, t, g0, g1)
            if s < PURIFY - 1:
                ga[s + 1].begin(t)
            else:
                put(t).start()

        if s < PURIFY - 1:
            z_own(s + 1, 0, "start")
    for s in range(PURIFY):
        for q in range(Q):
            z_drain(s, q)

        @pl.loop(0, T)
        def _(t):
            ga[s].drain(t)
            for q in range(Q):
                gs[s][q].drain(t)

    @pl.loop(0, T)
    def _(t):
        put(t).wait()


def on_device(dims, density, pattern, filters):
    nd, nr, nc, h, w, tm, cuts = dims
    Q = len(cuts)
    G = w // LANES
    J = nd * nc
    n_peers = J // CORES - 1
    T = h // tm
    dma = pltpu.SemaphoreType.DMA
    return pl.pallas_call(
        functools.partial(kernel, dims),
        out_shape=jax.ShapeDtypeStruct((h, w), jnp.float32),
        in_specs=[pl.BlockSpec(memory_space=pl.ANY)] * 3,
        out_specs=pl.BlockSpec(memory_space=pl.ANY),
        scratch_shapes=[
            pltpu.VMEM((PURIFY, J, G, h, LANES), jnp.bfloat16),
            pltpu.VMEM((PURIFY, nr, G, h, LANES), jnp.bfloat16),
            pltpu.VMEM((PURIFY, J, G, h, LANES), jnp.bfloat16),
            pltpu.VMEM((h, w), jnp.float32),
            pltpu.VMEM((h, w), jnp.float32),
            pltpu.VMEM((2 * PURIFY + 1, T * 8, w), jnp.float32),
            pltpu.VMEM(pattern.shape, jnp.int32), pltpu.VMEM(filters.shape, jnp.int32),
            dma((PURIFY, Q, nr, 2)), dma((PURIFY, Q, nr)),
            dma((PURIFY, T, n_peers, 2)), dma((PURIFY, T, n_peers, 2)),
            dma((PURIFY, T, n_peers + 1)), dma((PURIFY, T, n_peers + 1)),
            dma((PURIFY, Q, T, n_peers, 2)), dma((PURIFY, Q, T, n_peers, 2)),
            dma((PURIFY, Q, T, n_peers + 1)), dma((PURIFY, Q, T, n_peers + 1)),
            dma((T,)), dma((2,)),
        ],
        compiler_params=pltpu.CompilerParams(
            collective_id=0, has_side_effects=True, vmem_limit_bytes=62 * 2 ** 20),
    )(density, pattern, filters)


def solution(mesh):
    nd, nr, nc = mesh.shape["depth"], mesh.shape["row"], mesh.shape["col"]

    def run(density, pattern, filters):
        h, w = density.shape
        tm = 512 if h % 512 == 0 else h
        groups = w // LANES
        cuts = [(g, g + 1) for g in range(groups)]
        if groups >= 4:
            cuts = [(g, g + 2) for g in range(0, groups - 2, 2)] + cuts[groups - 2:]
        return on_device((nd, nr, nc, h, w, tm, tuple(cuts)), density, pattern, filters)

    return jax.shard_map(
        run,
        mesh=mesh,
        in_specs=(P("row", ("depth", "col")), P(), P()),
        out_specs=P("row", ("depth", "col")),
        check_vma=False,
    )
```

```python
import functools

import jax
import jax.numpy as jnp
from jax import lax
from jax.experimental import pallas as pl
from jax.experimental.pallas import tpu as pltpu
from jax.sharding import PartitionSpec as P

BLK = 64
PURIFY = 2
CORES = 2
LANES = 128
MESH = pl.DeviceIdType.MESH


def kernel(dims, dens, pat_in, filt_in, out, a_row, a_col, s_row, sq, acc, mask, pat, filt,
           z_send, z_recv, a_send, a_recv, af_send, af_recv,
           s_send, s_recv, sf_send, sf_recv, o_sem, t_sem):
    nd, nr, nc, h, w, tm, cuts = dims
    Q = len(cuts)
    G = w // LANES
    T = h // tm
    nx = nd // CORES
    m = h // w
    rb, sb = h // BLK, w // BLK
    d, r, c = lax.axis_index("depth"), lax.axis_index("row"), lax.axis_index("col")
    x, core = d // CORES, d % CORES
    sib = x * CORES + (1 - core)
    me = d * nc + c
    peers = [(px, pc) for px in range(nx) for pc in range(nc) if px or pc]
    direct = [p for p, (px, pc) in enumerate(peers) if not (px and pc)]
    bent = [p for p, (px, pc) in enumerate(peers) if px and pc]

    def dev(dd, rr, cc):
        return (dd, rr, cc)

    def peer_to(p):
        px, pc = peers[p]
        return ((x + px) % nx) * CORES + core, (c + pc) % nc

    def peer_from(p, k):
        px, pc = peers[p]
        return ((x + nx - px) % nx) * CORES + k, (c + nc - pc) % nc

    def load(t):
        rows = pl.ds(pl.multiple_of(t * tm, tm), tm)
        return pltpu.make_async_copy(dens.at[rows, :], acc.at[rows, :], o_sem.at[t])

    tables = [pltpu.make_async_copy(pat_in, pat, t_sem.at[0]), pltpu.make_async_copy(filt_in, filt, t_sem.at[1])]
    tables[0].start()
    for t in range(T):
        load(t).start()
    tables[1].start()
    bar = pltpu.get_barrier_semaphore()
    for p in direct:
        dd, cc = peer_to(p)
        pl.semaphore_signal(bar, inc=1, device_id=dev(dd, r, cc), device_id_type=MESH)
    pl.semaphore_signal(bar, inc=1, device_id=dev(sib, r, c), device_id_type=MESH)

    @pl.when(r > 0)
    def _():
        pl.semaphore_signal(bar, inc=1, device_id=dev(d, r - 1, c), device_id_type=MESH)

    @pl.when(r < nr - 1)
    def _():
        pl.semaphore_signal(bar, inc=1, device_id=dev(d, r + 1, c), device_id_type=MESH)

    tb = tm // BLK
    slot = lax.broadcasted_iota(jnp.int32, (T * 8, pat.shape[0]), 0)
    r_pick = (slot // 8 * tb + slot % 8 + r * rb
              == lax.broadcasted_iota(jnp.int32, (T * 8, pat.shape[0]), 1)).astype(jnp.float32)
    c_pick = ((lax.broadcasted_iota(jnp.int32, (pat.shape[1], w), 1) // BLK + me * sb)
              == lax.broadcasted_iota(jnp.int32, (pat.shape[1], w), 0)).astype(jnp.float32)

    def expand(k, table):
        rows = jnp.dot(r_pick, table.astype(jnp.float32), preferred_element_type=jnp.float32)
        mask[k] = jnp.dot(rows, c_pick, preferred_element_type=jnp.float32)

    tables[0].wait()
    expand(0, pat[...])

    def tile_mask(k, t, g0, g1):
        n = (g1 - g0) * LANES
        mk = mask[k, pl.ds(pl.multiple_of(t * 8, 8), 8), g0 * LANES:g1 * LANES][:tb]
        return jnp.broadcast_to(mk[:, None, :], (tb, BLK, n)).reshape(tm, n)

    def rows_of(t):
        return pl.ds(pl.multiple_of(t * tm, tm), tm)

    def operand(t, groups):
        for g in groups:
            v = (acc[rows_of(t), g * LANES:(g + 1) * LANES] * tile_mask(0, t, g, g + 1)).astype(jnp.bfloat16)
            a_col[0, r, g, rows_of(t), :] = v
            a_row[0, me, g, rows_of(t), :] = v

    @pl.loop(0, T)
    def _(t):
        load(t).wait()
        operand(t, range(*cuts[0]))

    near = jnp.minimum(r, 1) + jnp.minimum(nr - 1 - r, 1)
    for n in range(3):
        @pl.when(near == n)
        def _():
            pl.semaphore_wait(bar, len(direct) + 1 + n)

    def z_copy(s, q, src, up):
        ref = a_col.at[s, src, cuts[q][0]:cuts[q][1]]
        return pltpu.make_async_remote_copy(
            src_ref=ref, dst_ref=ref, send_sem=z_send.at[s, q, src, up],
            recv_sem=z_recv.at[s, q, src],
            device_id=dev(d, r + 1 if up else r - 1, c), device_id_type=MESH)

    def z_own(s, q, op):
        @pl.when(r < nr - 1)
        def _():
            getattr(z_copy(s, q, r, 1), op)()

        @pl.when(r > 0)
        def _():
            getattr(z_copy(s, q, r, 0), op)()

    def pass_down(s, q, dist):
        z_copy(s, q, r + dist, 1).wait_recv()
        z_copy(s, q, r + dist, 0).start()

    def pass_up(s, q, dist):
        z_copy(s, q, r - dist, 0).wait_recv()
        z_copy(s, q, r - dist, 1).start()

    def z_fwd(s, q, dist, outer):
        for edge in (0, 1):
            if edge == outer:
                @pl.when((r + dist < nr) & (r > 0) & ((r + dist == nr - 1) == bool(edge)))
                def _():
                    pass_down(s, q, dist)

                @pl.when((r - dist >= 0) & (r < nr - 1) & ((r - dist == 0) == bool(edge)))
                def _():
                    pass_up(s, q, dist)

    def z_inner(s, q):
        for dist in range(1, nr - 1):
            z_fwd(s, q, dist, 0)

    def z_outer(s, q):
        for dist in range(1, nr - 1):
            z_fwd(s, q, dist, 1)

    def z_wait(s, q, dists=range(1, nr)):
        for dist in dists:
            @pl.when((r + dist < nr) & (r == 0))
            def _():
                z_copy(s, q, r + dist, 1).wait_recv()

            @pl.when((r - dist >= 0) & (r == nr - 1))
            def _():
                z_copy(s, q, r - dist, 0).wait_recv()

    def z_drain(s, q):
        z_own(s, q, "wait_send")
        for dist in range(1, nr - 1):
            @pl.when((r + dist < nr) & (r > 0))
            def _():
                z_copy(s, q, r + dist, 0).wait_send()

            @pl.when((r - dist >= 0) & (r < nr - 1))
            def _():
                z_copy(s, q, r - dist, 1).wait_send()

    def ac(ref, ss, rs, to):
        return pltpu.make_async_remote_copy(
            src_ref=ref, dst_ref=ref, send_sem=ss, recv_sem=rs,
            device_id=dev(to[0], r, to[1]), device_id_type=MESH)

    class Gather:
        def __init__(self, view, sems, tag):
            self.view, self.sems, self.tag = view, sems, tag

        def sem(self, n, t, *at):
            return self.sems[n].at[(*self.tag, t, *at)]

        def block(self, p, k, t):
            dd, cc = peer_from(p, k)
            return self.view(dd * nc + cc, t * tm, tm)

        def half(self, dd, cc, t, i):
            return self.view(dd * nc + cc, t * tm + i * (tm // 2), tm // 2)

        def path(self, ref, p, t, i, to):
            return ac(ref, self.sem(0, t, p, i), self.sem(1, t, p, i), to)

        def own(self, p, t):
            return self.path(self.view(me, t * tm, tm), p, t, 0, peer_to(p))

        def got(self, p, t, i=None):
            if i is None:
                return self.path(self.block(p, core, t), p, t, 0, peer_to(p))
            dd, cc = peer_from(p, core)
            return self.path(self.half(dd, cc, t, i), p, t, i, peer_to(p))

        def turn(self, p, t, i):
            px, pc = peers[p]
            if i == 0:
                ref = self.half(((x + nx - px) % nx) * CORES + core, c, t, 0)
                to = (d, (c + pc) % nc)
            else:
                ref = self.half(d, (c + nc - pc) % nc, t, 1)
                to = (((x + px) % nx) * CORES + core, c)
            return self.path(ref, p, t, i, to)

        def fwd(self, p, t):
            ref = self.view(me, t * tm, tm) if p == len(peers) else self.block(p, core, t)
            return ac(ref, self.sem(2, t, p), self.sem(3, t, p), (sib, c))

        def fgot(self, p, t):
            ref = self.view(sib * nc + c, t * tm, tm) if p == len(peers) else self.block(p, 1 - core, t)
            return ac(ref, self.sem(2, t, p), self.sem(3, t, p), (sib, c))

        def begin(self, t):
            for p in direct:
                self.own(p, t).start()
            self.fwd(len(peers), t).start()

        def hop(self, t):
            for q in direct:
                self.got(q, t).wait_recv()
                for p in bent:
                    if peers[q] == (peers[p][0], 0):
                        self.turn(p, t, 0).start()
                    if peers[q] == (0, peers[p][1]):
                        self.turn(p, t, 1).start()
            for q in direct:
                self.fwd(q, t).start()

        def relay(self, t):
            for p in bent:
                self.got(p, t, 0).wait_recv()
                self.got(p, t, 1).wait_recv()
                self.fwd(p, t).start()

        def finish(self, t):
            for p in range(len(peers) + 1):
                self.fgot(p, t).wait_recv()

        def drain(self, t):
            for p in direct:
                self.own(p, t).wait_send()
            for p in bent:
                self.turn(p, t, 0).wait_send()
                self.turn(p, t, 1).wait_send()
            for p in range(len(peers) + 1):
                self.fwd(p, t).wait_send()

    def span(lo, n):
        return pl.ds(lo if isinstance(lo, int) else pl.multiple_of(lo, tm // 2), n)

    ga = [Gather(lambda j, lo, n, s=s: a_row.at[s, j, :, span(lo, n)],
                 (a_send, a_recv, af_send, af_recv), (s,)) for s in range(PURIFY)]
    gs = [[Gather(lambda j, lo, n, s=s, q=q: s_row.at[s, j, cuts[q][0]:cuts[q][1], span(lo, n)],
                  (s_send, s_recv, sf_send, sf_recv), (s, q)) for q in range(Q)] for s in range(PURIFY)]

    last = jnp.where(r < nr // 2, nr - 1, 0)
    early = [i for i in range(nr * m) if i < (nr - 1) * m]
    late = [i for i in range(nr * m) if i >= (nr - 1) * m]

    def product(left, s, t, groups, g0, g1, part=None):
        if part is None:
            cells = [(j, g) for j in range(nd * nc) for g in groups]
        else:
            first = lax.rem(last + 1, nr) * m
            cells = [(lax.rem(first + i, nr * m), g) for i in part for g in groups]
        tot = None
        for i in range(0, len(cells), 2):
            pair = cells[i:i + 2]
            lhs = jnp.concatenate([left[s, j, g, rows_of(t), :] for j, g in pair], axis=1)
            cols = []
            for n in range(g0, g1):
                los = [(j // m, (j % m) * w + g * LANES) for j, g in pair]
                if part is not None:
                    los = [(b, pl.multiple_of(lo, LANES)) for b, lo in los]
                if len(los) == 2 and (pair[0][0] is pair[1][0] or part is None) and pair[1] == (pair[0][0], pair[0][1] + 1):
                    cols.append(a_col[s, los[0][0], n, pl.ds(los[0][1], 2 * LANES), :])
                else:
                    cols.append(jnp.concatenate([a_col[s, b, n, pl.ds(lo, LANES), :] for b, lo in los], axis=0))
            term = jnp.dot(lhs, jnp.concatenate(cols, axis=1), preferred_element_type=jnp.float32)
            tot = term if tot is None else tot + term
        return tot

    def begun(s, q, t):
        g0, g1 = cuts[q]
        sq[rows_of(t), g0 * LANES:g1 * LANES] = product(a_row, s, t, range(G), g0, g1, early)

    def square(s, q, t, split=False):
        g0, g1 = cuts[q]
        if split:
            tot = product(a_row, s, t, range(G), g0, g1, late) + sq[rows_of(t), g0 * LANES:g1 * LANES]
        else:
            tot = product(a_row, s, t, range(G), g0, g1)
        tot = tot * tile_mask(2 * s + 1, t, g0, g1)
        sq[rows_of(t), g0 * LANES:g1 * LANES] = tot
        v = tot.astype(jnp.bfloat16)
        for g in range(g0, g1):
            s_row[s, me, g, rows_of(t), :] = v[:, (g - g0) * LANES:(g - g0 + 1) * LANES]

    def put(t):
        return pltpu.make_async_copy(acc.at[rows_of(t), :], out.at[rows_of(t), :], o_sem.at[t])

    def cubic(s, k, t, g0, g1):
        cols = slice(g0 * LANES, g1 * LANES)
        tot = product(s_row, s, t, range(*cuts[k]), g0, g1)
        if k > 0:
            tot = tot + acc[rows_of(t), cols]
        if k < Q - 1:
            acc[rows_of(t), cols] = tot
            return
        cur = 3.0 * sq[rows_of(t), cols] - 2.0 * (tot * tile_mask(2 * s + 2, t, g0, g1))
        if s < PURIFY - 1:
            v = cur.astype(jnp.bfloat16)
            for g in range(g0, g1):
                part = v[:, (g - g0) * LANES:(g - g0 + 1) * LANES]
                a_col[s + 1, r, g, rows_of(t), :] = part
                a_row[s + 1, me, g, rows_of(t), :] = part
        else:
            acc[rows_of(t), cols] = cur

    wide = [(g, min(g + 2, G)) for g in range(0, G, 2)]
    ready = [[] for _ in range(Q)]
    for k in range(Q - 1):
        for g0, g1 in wide:
            ready[next(q for q in range(k + 1, Q) if q == Q - 1 or cuts[q][1] >= g1)].append((k, (g0, g1)))
    z_own(0, 0, "start")

    @pl.loop(0, T)
    def _(t):
        operand(t, range(cuts[0][1], G))
        ga[0].begin(t)

    tables[1].wait()
    for k in range(filt.shape[0]):
        expand(k + 1, filt[k])
    for s in range(PURIFY):
        ga[s].hop(0)
        z_inner(s, 0)
        if Q > 1 and s > 0:
            z_own(s, 1, "start")
        z_outer(s, 0)
        if Q > 1 and s == 0:
            z_own(s, 1, "start")
        for t in range(1, T):
            ga[s].hop(t)
        if Q > 1:
            z_inner(s, 1)
        for t in range(T):
            ga[s].relay(t)
        if Q > 1:
            z_outer(s, 1)
        if Q > 2:
            z_own(s, 2, "start")
        z_wait(s, 0)

        @pl.loop(0, T)
        def _(t):
            ga[s].finish(t)
            square(s, 0, t)
            gs[s][0].begin(t)

        for q in range(1, Q):
            if q + 1 < Q:
                z_inner(s, q + 1)
                z_outer(s, q + 1)
                if q + 2 < Q:
                    z_own(s, q + 2, "start")

            @pl.loop(0, T)
            def _(t):
                gs[s][q - 1].hop(t)

            split = q == Q - 1
            if split:
                z_wait(s, q, range(1, nr - 1))

                @pl.loop(0, T)
                def _(t):
                    begun(s, q, t)

                z_wait(s, q, (nr - 1,))
            else:
                z_wait(s, q)

            @pl.loop(0, T)
            def _(t):
                square(s, q, t, split)
                gs[s][q].begin(t)

            @pl.loop(0, T)
            def _(t):
                gs[s][q - 1].relay(t)

            @pl.loop(0, T)
            def _(t):
                gs[s][q - 1].finish(t)
                for k, (g0, g1) in ready[q]:
                    cubic(s, k, t, g0, g1)

        @pl.loop(0, T)
        def _(t):
            gs[s][Q - 1].hop(t)

        @pl.loop(0, T)
        def _(t):
            gs[s][Q - 1].relay(t)
            gs[s][Q - 1].finish(t)
            for g0, g1 in wide:
                cubic(s, Q - 1, t, g0, g1)
            if s < PURIFY - 1:
                ga[s + 1].begin(t)
            else:
                put(t).start()

        if s < PURIFY - 1:
            z_own(s + 1, 0, "start")
    for s in range(PURIFY):
        for q in range(Q):
            z_drain(s, q)

        @pl.loop(0, T)
        def _(t):
            ga[s].drain(t)
            for q in range(Q):
                gs[s][q].drain(t)

    @pl.loop(0, T)
    def _(t):
        put(t).wait()


def on_device(dims, density, pattern, filters):
    nd, nr, nc, h, w, tm, cuts = dims
    Q = len(cuts)
    G = w // LANES
    J = nd * nc
    n_peers = J // CORES - 1
    T = h // tm
    dma = pltpu.SemaphoreType.DMA
    return pl.pallas_call(
        functools.partial(kernel, dims),
        out_shape=jax.ShapeDtypeStruct((h, w), jnp.float32),
        in_specs=[pl.BlockSpec(memory_space=pl.ANY)] * 3,
        out_specs=pl.BlockSpec(memory_space=pl.ANY),
        scratch_shapes=[
            pltpu.VMEM((PURIFY, J, G, h, LANES), jnp.bfloat16),
            pltpu.VMEM((PURIFY, nr, G, h, LANES), jnp.bfloat16),
            pltpu.VMEM((PURIFY, J, G, h, LANES), jnp.bfloat16),
            pltpu.VMEM((h, w), jnp.float32),
            pltpu.VMEM((h, w), jnp.float32),
            pltpu.VMEM((2 * PURIFY + 1, T * 8, w), jnp.float32),
            pltpu.VMEM(pattern.shape, jnp.int32), pltpu.VMEM(filters.shape, jnp.int32),
            dma((PURIFY, Q, nr, 2)), dma((PURIFY, Q, nr)),
            dma((PURIFY, T, n_peers, 2)), dma((PURIFY, T, n_peers, 2)),
            dma((PURIFY, T, n_peers + 1)), dma((PURIFY, T, n_peers + 1)),
            dma((PURIFY, Q, T, n_peers, 2)), dma((PURIFY, Q, T, n_peers, 2)),
            dma((PURIFY, Q, T, n_peers + 1)), dma((PURIFY, Q, T, n_peers + 1)),
            dma((T,)), dma((2,)),
        ],
        compiler_params=pltpu.CompilerParams(
            collective_id=0, has_side_effects=True, vmem_limit_bytes=62 * 2 ** 20),
    )(density, pattern, filters)


def solution(mesh):
    nd, nr, nc = mesh.shape["depth"], mesh.shape["row"], mesh.shape["col"]

    def run(density, pattern, filters):
        h, w = density.shape
        tm = 512 if h % 512 == 0 else h
        groups = w // LANES
        cuts = [(g, g + 1) for g in range(groups)]
        if groups >= 4:
            cuts = [(g, g + 2) for g in range(0, groups - 2, 2)] + cuts[groups - 2:]
        return on_device((nd, nr, nc, h, w, tm, tuple(cuts)), density, pattern, filters)

    return jax.shard_map(
        run,
        mesh=mesh,
        in_specs=(P("row", ("depth", "col")), P(), P()),
        out_specs=P("row", ("depth", "col")),
        check_vma=False,
    )
```

```python
import functools

import jax
import jax.numpy as jnp
from jax import lax
from jax.experimental import pallas as pl
from jax.experimental.pallas import tpu as pltpu
from jax.sharding import PartitionSpec as P

BLK = 64
PURIFY = 2
CORES = 2
LANES = 128
MESH = pl.DeviceIdType.MESH


def kernel(dims, dens, pat_in, filt_in, out, a_row, a_col, s_row, sq, acc, mask, pat, filt,
           z_send, z_recv, a_send, a_recv, af_send, af_recv,
           s_send, s_recv, sf_send, sf_recv, o_sem, t_sem, res):
    nd, nr, nc, h, w, tm, cuts = dims
    Q = len(cuts)
    G = w // LANES
    T = h // tm
    nx = nd // CORES
    m = h // w
    rb, sb = h // BLK, w // BLK
    d, r, c = lax.axis_index("depth"), lax.axis_index("row"), lax.axis_index("col")
    x, core = d // CORES, d % CORES
    sib = x * CORES + (1 - core)
    me = d * nc + c
    peers = [(px, pc) for px in range(nx) for pc in range(nc) if px or pc]
    direct = [p for p, (px, pc) in enumerate(peers) if not (px and pc)]
    bent = [p for p, (px, pc) in enumerate(peers) if px and pc]

    def dev(dd, rr, cc):
        return (dd, rr, cc)

    def peer_to(p):
        px, pc = peers[p]
        return ((x + px) % nx) * CORES + core, (c + pc) % nc

    def peer_from(p, k):
        px, pc = peers[p]
        return ((x + nx - px) % nx) * CORES + k, (c + nc - pc) % nc

    def load(t):
        rows = pl.ds(pl.multiple_of(t * tm, tm), tm)
        return pltpu.make_async_copy(dens.at[rows, :], acc.at[rows, :], o_sem.at[t])

    tables = [pltpu.make_async_copy(pat_in, pat, t_sem.at[0]), pltpu.make_async_copy(filt_in, filt, t_sem.at[1])]
    tables[0].start()
    for t in range(T):
        load(t).start()
    tables[1].start()
    bar = pltpu.get_barrier_semaphore()
    for p in direct:
        dd, cc = peer_to(p)
        pl.semaphore_signal(bar, inc=1, device_id=dev(dd, r, cc), device_id_type=MESH)
    pl.semaphore_signal(bar, inc=1, device_id=dev(sib, r, c), device_id_type=MESH)

    @pl.when(r > 0)
    def _():
        pl.semaphore_signal(bar, inc=1, device_id=dev(d, r - 1, c), device_id_type=MESH)

    @pl.when(r < nr - 1)
    def _():
        pl.semaphore_signal(bar, inc=1, device_id=dev(d, r + 1, c), device_id_type=MESH)

    tb = tm // BLK
    slot = lax.broadcasted_iota(jnp.int32, (T * 8, pat.shape[0]), 0)
    r_pick = (slot // 8 * tb + slot % 8 + r * rb
              == lax.broadcasted_iota(jnp.int32, (T * 8, pat.shape[0]), 1)).astype(jnp.float32)
    c_pick = ((lax.broadcasted_iota(jnp.int32, (pat.shape[1], w), 1) // BLK + me * sb)
              == lax.broadcasted_iota(jnp.int32, (pat.shape[1], w), 0)).astype(jnp.float32)

    def expand(k, table):
        rows = jnp.dot(r_pick, table.astype(jnp.float32), preferred_element_type=jnp.float32)
        mask[k] = jnp.dot(rows, c_pick, preferred_element_type=jnp.float32)

    tables[0].wait()
    expand(0, pat[...])

    def tile_mask(k, t, g0, g1):
        n = (g1 - g0) * LANES
        mk = mask[k, pl.ds(pl.multiple_of(t * 8, 8), 8), g0 * LANES:g1 * LANES][:tb]
        return jnp.broadcast_to(mk[:, None, :], (tb, BLK, n)).reshape(tm, n)

    def rows_of(t):
        return pl.ds(pl.multiple_of(t * tm, tm), tm)

    def operand(t, groups):
        for g in groups:
            v = (acc[rows_of(t), g * LANES:(g + 1) * LANES] * tile_mask(0, t, g, g + 1)).astype(jnp.bfloat16)
            a_col[0, r, g, rows_of(t), :] = v
            a_row[0, me, g, rows_of(t), :] = v

    @pl.loop(0, T)
    def _(t):
        load(t).wait()
        operand(t, range(*cuts[0]))

    near = jnp.minimum(r, 1) + jnp.minimum(nr - 1 - r, 1)
    for n in range(3):
        @pl.when(near == n)
        def _():
            pl.semaphore_wait(bar, len(direct) + 1 + n)

    def z_copy(s, q, src, up):
        ref = a_col.at[s, src, cuts[q][0]:cuts[q][1]]
        return pltpu.make_async_remote_copy(
            src_ref=ref, dst_ref=ref, send_sem=z_send.at[s, q, src, up],
            recv_sem=z_recv.at[s, q, src],
            device_id=dev(d, r + 1 if up else r - 1, c), device_id_type=MESH)

    def z_own(s, q, op):
        @pl.when(r < nr - 1)
        def _():
            getattr(z_copy(s, q, r, 1), op)()

        @pl.when(r > 0)
        def _():
            getattr(z_copy(s, q, r, 0), op)()

    def pass_down(s, q, dist):
        z_copy(s, q, r + dist, 1).wait_recv()
        z_copy(s, q, r + dist, 0).start()

    def pass_up(s, q, dist):
        z_copy(s, q, r - dist, 0).wait_recv()
        z_copy(s, q, r - dist, 1).start()

    def z_fwd(s, q, dist, outer):
        for edge in (0, 1):
            if edge == outer:
                @pl.when((r + dist < nr) & (r > 0) & ((r + dist == nr - 1) == bool(edge)))
                def _():
                    pass_down(s, q, dist)

                @pl.when((r - dist >= 0) & (r < nr - 1) & ((r - dist == 0) == bool(edge)))
                def _():
                    pass_up(s, q, dist)

    def z_inner(s, q):
        for dist in range(1, nr - 1):
            z_fwd(s, q, dist, 0)

    def z_outer(s, q):
        for dist in range(1, nr - 1):
            z_fwd(s, q, dist, 1)

    def z_wait(s, q, dists=range(1, nr)):
        for dist in dists:
            @pl.when((r + dist < nr) & (r == 0))
            def _():
                z_copy(s, q, r + dist, 1).wait_recv()

            @pl.when((r - dist >= 0) & (r == nr - 1))
            def _():
                z_copy(s, q, r - dist, 0).wait_recv()

    def z_drain(s, q):
        z_own(s, q, "wait_send")
        for dist in range(1, nr - 1):
            @pl.when((r + dist < nr) & (r > 0))
            def _():
                z_copy(s, q, r + dist, 0).wait_send()

            @pl.when((r - dist >= 0) & (r < nr - 1))
            def _():
                z_copy(s, q, r - dist, 1).wait_send()

    def ac(ref, ss, rs, to):
        return pltpu.make_async_remote_copy(
            src_ref=ref, dst_ref=ref, send_sem=ss, recv_sem=rs,
            device_id=dev(to[0], r, to[1]), device_id_type=MESH)

    class Gather:
        def __init__(self, view, sems, tag):
            self.view, self.sems, self.tag = view, sems, tag

        def sem(self, n, t, *at):
            return self.sems[n].at[(*self.tag, t, *at)]

        def block(self, p, k, t):
            dd, cc = peer_from(p, k)
            return self.view(dd * nc + cc, t * tm, tm)

        def half(self, dd, cc, t, i):
            return self.view(dd * nc + cc, t * tm + i * (tm // 2), tm // 2)

        def path(self, ref, p, t, i, to):
            return ac(ref, self.sem(0, t, p, i), self.sem(1, t, p, i), to)

        def own(self, p, t):
            return self.path(self.view(me, t * tm, tm), p, t, 0, peer_to(p))

        def got(self, p, t, i=None):
            if i is None:
                return self.path(self.block(p, core, t), p, t, 0, peer_to(p))
            dd, cc = peer_from(p, core)
            return self.path(self.half(dd, cc, t, i), p, t, i, peer_to(p))

        def turn(self, p, t, i):
            px, pc = peers[p]
            if i == 0:
                ref = self.half(((x + nx - px) % nx) * CORES + core, c, t, 0)
                to = (d, (c + pc) % nc)
            else:
                ref = self.half(d, (c + nc - pc) % nc, t, 1)
                to = (((x + px) % nx) * CORES + core, c)
            return self.path(ref, p, t, i, to)

        def fwd(self, p, t):
            ref = self.view(me, t * tm, tm) if p == len(peers) else self.block(p, core, t)
            return ac(ref, self.sem(2, t, p), self.sem(3, t, p), (sib, c))

        def fgot(self, p, t):
            ref = self.view(sib * nc + c, t * tm, tm) if p == len(peers) else self.block(p, 1 - core, t)
            return ac(ref, self.sem(2, t, p), self.sem(3, t, p), (sib, c))

        def begin(self, t):
            for p in direct:
                self.own(p, t).start()
            self.fwd(len(peers), t).start()

        def hop(self, t):
            for q in direct:
                self.got(q, t).wait_recv()
                for p in bent:
                    if peers[q] == (peers[p][0], 0):
                        self.turn(p, t, 0).start()
                    if peers[q] == (0, peers[p][1]):
                        self.turn(p, t, 1).start()
            for q in direct:
                self.fwd(q, t).start()

        def relay(self, t):
            for p in bent:
                self.got(p, t, 0).wait_recv()
                self.got(p, t, 1).wait_recv()
                self.fwd(p, t).start()

        def finish(self, t):
            for p in range(len(peers) + 1):
                self.fgot(p, t).wait_recv()

        def drain(self, t):
            for p in direct:
                self.own(p, t).wait_send()
            for p in bent:
                self.turn(p, t, 0).wait_send()
                self.turn(p, t, 1).wait_send()
            for p in range(len(peers) + 1):
                self.fwd(p, t).wait_send()

    def span(lo, n):
        return pl.ds(lo if isinstance(lo, int) else pl.multiple_of(lo, tm // 2), n)

    ga = [Gather(lambda j, lo, n, s=s: a_row.at[s, j, :, span(lo, n)],
                 (a_send, a_recv, af_send, af_recv), (s,)) for s in range(PURIFY)]
    gs = [[Gather(lambda j, lo, n, s=s, q=q: s_row.at[s, j, cuts[q][0]:cuts[q][1], span(lo, n)],
                  (s_send, s_recv, sf_send, sf_recv), (s, q)) for q in range(Q)] for s in range(PURIFY)]

    last = jnp.where(r < nr // 2, nr - 1, 0)
    early = [i for i in range(nr * m) if i < (nr - 1) * m]
    late = [i for i in range(nr * m) if i >= (nr - 1) * m]

    def product(left, s, t, groups, g0, g1, part=None):
        if part is None:
            cells = [(j, g) for j in range(nd * nc) for g in groups]
        else:
            first = lax.rem(last + 1, nr) * m
            cells = [(lax.rem(first + i, nr * m), g) for i in part for g in groups]
        tot = None
        for i in range(0, len(cells), 2):
            pair = cells[i:i + 2]
            lhs = jnp.concatenate([left[s, j, g, rows_of(t), :] for j, g in pair], axis=1)
            cols = []
            for n in range(g0, g1):
                los = [(j // m, (j % m) * w + g * LANES) for j, g in pair]
                if part is not None:
                    los = [(b, pl.multiple_of(lo, LANES)) for b, lo in los]
                if len(los) == 2 and (pair[0][0] is pair[1][0] or part is None) and pair[1] == (pair[0][0], pair[0][1] + 1):
                    cols.append(a_col[s, los[0][0], n, pl.ds(los[0][1], 2 * LANES), :])
                else:
                    cols.append(jnp.concatenate([a_col[s, b, n, pl.ds(lo, LANES), :] for b, lo in los], axis=0))
            term = jnp.dot(lhs, jnp.concatenate(cols, axis=1), preferred_element_type=jnp.float32)
            tot = term if tot is None else tot + term
        return tot

    def begun(s, q, t):
        g0, g1 = cuts[q]
        sq[rows_of(t), g0 * LANES:g1 * LANES] = product(a_row, s, t, range(G), g0, g1, early)

    def square(s, q, t, split=False):
        g0, g1 = cuts[q]
        if split:
            tot = product(a_row, s, t, range(G), g0, g1, late) + sq[rows_of(t), g0 * LANES:g1 * LANES]
        else:
            tot = product(a_row, s, t, range(G), g0, g1)
        tot = tot * tile_mask(2 * s + 1, t, g0, g1)
        sq[rows_of(t), g0 * LANES:g1 * LANES] = tot
        v = tot.astype(jnp.bfloat16)
        for g in range(g0, g1):
            s_row[s, me, g, rows_of(t), :] = v[:, (g - g0) * LANES:(g - g0 + 1) * LANES]

    def put(t):
        return pltpu.make_async_copy(res.at[rows_of(t), :], out.at[rows_of(t), :], o_sem.at[t])

    def cubic(s, k, t, g0, g1):
        cols = slice(g0 * LANES, g1 * LANES)
        tot = product(s_row, s, t, range(*cuts[k]), g0, g1)
        if k > 0:
            tot = tot + acc[rows_of(t), cols]
        if k < Q - 1:
            acc[rows_of(t), cols] = tot
            return
        cur = 3.0 * sq[rows_of(t), cols] - 2.0 * (tot * tile_mask(2 * s + 2, t, g0, g1))
        if s < PURIFY - 1:
            v = cur.astype(jnp.bfloat16)
            for g in range(g0, g1):
                part = v[:, (g - g0) * LANES:(g - g0 + 1) * LANES]
                a_col[s + 1, r, g, rows_of(t), :] = part
                a_row[s + 1, me, g, rows_of(t), :] = part
        else:
            res[rows_of(t), cols] = cur.astype(jnp.bfloat16)

    wide = [(g, min(g + 2, G)) for g in range(0, G, 2)]
    ready = [[] for _ in range(Q)]
    for k in range(Q - 1):
        for g0, g1 in wide:
            ready[next(q for q in range(k + 1, Q) if q == Q - 1 or cuts[q][1] >= g1)].append((k, (g0, g1)))
    z_own(0, 0, "start")

    @pl.loop(0, T)
    def _(t):
        operand(t, range(cuts[0][1], G))
        ga[0].begin(t)

    tables[1].wait()
    for k in range(filt.shape[0]):
        expand(k + 1, filt[k])
    for s in range(PURIFY):
        ga[s].hop(0)
        z_inner(s, 0)
        if Q > 1 and s > 0:
            z_own(s, 1, "start")
        z_outer(s, 0)
        if Q > 1 and s == 0:
            z_own(s, 1, "start")
        for t in range(1, T):
            ga[s].hop(t)
        if Q > 1:
            z_inner(s, 1)
        for t in range(T):
            ga[s].relay(t)
        if Q > 1:
            z_outer(s, 1)
        if Q > 2:
            z_own(s, 2, "start")
        z_wait(s, 0)

        @pl.loop(0, T)
        def _(t):
            ga[s].finish(t)
            square(s, 0, t)
            gs[s][0].begin(t)

        for q in range(1, Q):
            if q + 1 < Q:
                z_inner(s, q + 1)
                z_outer(s, q + 1)
                if q + 2 < Q:
                    z_own(s, q + 2, "start")

            @pl.loop(0, T)
            def _(t):
                gs[s][q - 1].hop(t)

            split = q == Q - 1
            if split:
                z_wait(s, q, range(1, nr - 1))

                @pl.loop(0, T)
                def _(t):
                    begun(s, q, t)

                z_wait(s, q, (nr - 1,))
            else:
                z_wait(s, q)

            @pl.loop(0, T)
            def _(t):
                square(s, q, t, split)
                gs[s][q].begin(t)

            @pl.loop(0, T)
            def _(t):
                gs[s][q - 1].relay(t)

            @pl.loop(0, T)
            def _(t):
                gs[s][q - 1].finish(t)
                for k, (g0, g1) in ready[q]:
                    cubic(s, k, t, g0, g1)

        @pl.loop(0, T)
        def _(t):
            gs[s][Q - 1].hop(t)

        @pl.loop(0, T)
        def _(t):
            gs[s][Q - 1].relay(t)
            gs[s][Q - 1].finish(t)
            for g0, g1 in wide:
                cubic(s, Q - 1, t, g0, g1)
            if s < PURIFY - 1:
                ga[s + 1].begin(t)
            else:
                put(t).start()

        if s < PURIFY - 1:
            z_own(s + 1, 0, "start")
    for s in range(PURIFY):
        for q in range(Q):
            z_drain(s, q)

        @pl.loop(0, T)
        def _(t):
            ga[s].drain(t)
            for q in range(Q):
                gs[s][q].drain(t)

    @pl.loop(0, T)
    def _(t):
        put(t).wait()


def on_device(dims, density, pattern, filters):
    nd, nr, nc, h, w, tm, cuts = dims
    Q = len(cuts)
    G = w // LANES
    J = nd * nc
    n_peers = J // CORES - 1
    T = h // tm
    dma = pltpu.SemaphoreType.DMA
    return pl.pallas_call(
        functools.partial(kernel, dims),
        out_shape=jax.ShapeDtypeStruct((h, w), jnp.bfloat16),
        in_specs=[pl.BlockSpec(memory_space=pl.ANY)] * 3,
        out_specs=pl.BlockSpec(memory_space=pl.ANY),
        scratch_shapes=[
            pltpu.VMEM((PURIFY, J, G, h, LANES), jnp.bfloat16),
            pltpu.VMEM((PURIFY, nr, G, h, LANES), jnp.bfloat16),
            pltpu.VMEM((PURIFY, J, G, h, LANES), jnp.bfloat16),
            pltpu.VMEM((h, w), jnp.float32),
            pltpu.VMEM((h, w), jnp.float32),
            pltpu.VMEM((2 * PURIFY + 1, T * 8, w), jnp.float32),
            pltpu.VMEM(pattern.shape, jnp.int32), pltpu.VMEM(filters.shape, jnp.int32),
            dma((PURIFY, Q, nr, 2)), dma((PURIFY, Q, nr)),
            dma((PURIFY, T, n_peers, 2)), dma((PURIFY, T, n_peers, 2)),
            dma((PURIFY, T, n_peers + 1)), dma((PURIFY, T, n_peers + 1)),
            dma((PURIFY, Q, T, n_peers, 2)), dma((PURIFY, Q, T, n_peers, 2)),
            dma((PURIFY, Q, T, n_peers + 1)), dma((PURIFY, Q, T, n_peers + 1)),
            dma((T,)), dma((2,)), pltpu.VMEM((h, w), jnp.bfloat16),
        ],
        compiler_params=pltpu.CompilerParams(
            collective_id=0, has_side_effects=True, vmem_limit_bytes=62 * 2 ** 20),
    )(density, pattern, filters).astype(jnp.float32)


def solution(mesh):
    nd, nr, nc = mesh.shape["depth"], mesh.shape["row"], mesh.shape["col"]

    def run(density, pattern, filters):
        h, w = density.shape
        tm = 512 if h % 512 == 0 else h
        groups = w // LANES
        cuts = [(g, g + 1) for g in range(groups)]
        if groups >= 4:
            cuts = [(g, g + 2) for g in range(0, groups - 2, 2)] + cuts[groups - 2:]
        return on_device((nd, nr, nc, h, w, tm, tuple(cuts)), density, pattern, filters)

    return jax.shard_map(
        run,
        mesh=mesh,
        in_specs=(P("row", ("depth", "col")), P(), P()),
        out_specs=P("row", ("depth", "col")),
        check_vma=False,
    )
```
